32 devices in a mesh: batch: 4 (over z), mp: 8 (over y, x, core).
Axes of the slice: x: 2, y: 2, z: 4, core: 2. Of those that a mesh axis runs over, the one named last changes fastest.
Arguments:
- hidden_in: bfloat16 [128, 16384], P('batch'), may hold values from -36 to 36
- queries: bfloat16 [128, 16384], P('batch', 'mp'), may hold values from -128 to 128
- key_cache: bfloat16 [128, 1024], P('batch'), may hold values from -4.5 to 4.5
- value_cache: bfloat16 [128, 1024], P('batch'), may hold values from -4 to 4
- question: int32 [32], P('batch'), may hold values from 0 to 3
- prefix_len: int32 [4], replicated, may hold values from 6 to 24, as said below
- norm_gain: float32 [16384], replicated, may hold values from 0.1 to 1.9
- gate_weight: bfloat16 [16384, 26624], P('batch', 'mp'), may hold values from -0.046875 to 0.046875
- up_weight: bfloat16 [16384, 26624], P('batch', 'mp'), may hold values from -0.046875 to 0.046875
- down_weight: bfloat16 [26624, 16384], P('mp', 'batch'), may hold values from -0.0390625 to 0.0390625
Outputs:
- layer_out: bfloat16 [128, 16384], P('mp', 'batch')
The draws below stay inside these ranges and needn't reach their ends.
Inputs may be any that keep to these rules, and one draw needn't show every extreme that they name: `prefix_len`: some question has all 24 prefix tokens live, and another question has the fewest allowed.
All inputs are finite; a program needn't handle non-finite values.
Results may differ from the reference program's by a relative error of at most 0.0055.
Values may be sent and summed in bfloat16 or wider, within the bound.
A program may use at most 128 MiB of HBM per device.

```python
import math
import jax
import jax.numpy as jnp
from jax import lax

D = 16384
HEADS = 128
KV_HEADS = 8
HEAD_DIM = 128
FF = 26624
PREFIX = 24
OPT_DEV = 8
ROWS_DEV = 32
QUESTIONS = 4
OPTIONS = 32
ROWS = 128
KV_WIDTH = 1024


def shared_keys(key):
    return jax.random.truncated_normal(jax.random.fold_in(key, 101), -4.0, 4.0, (ROWS, KV_WIDTH), jnp.float32)


def shared_map(key):
    return jax.random.randint(jax.random.fold_in(key, 103), (OPTIONS,), 0, QUESTIONS).astype(jnp.int32)


def draw_key_cache(key, part):
    drawn = shared_keys(key)
    return drawn.astype(jnp.bfloat16)


def draw_queries(key, part):
    key = jax.random.fold_in(key, 7)
    queries = jax.random.truncated_normal(key, -4.0, 4.0, (ROWS, D), jnp.float32)
    return queries.astype(jnp.bfloat16)


def draw_question(key, part):
    return shared_map(key)


def draw_prefix_len(key, part):
    key = jax.random.fold_in(key, 11)
    first_key, second_key, third_key = jax.random.split(key, 3)
    fewest = max(2, PREFIX // 4)
    lengths = jax.random.randint(first_key, (QUESTIONS,), fewest, PREFIX + 1)
    chosen = jax.random.randint(second_key, (), 0, QUESTIONS)
    other = (chosen + 1 + jax.random.randint(third_key, (), 0, QUESTIONS - 1)) % QUESTIONS
    positions = jnp.arange(QUESTIONS)
    lengths = jnp.where(positions == other, fewest, lengths)
    return jnp.where(positions == chosen, PREFIX, lengths).astype(jnp.int32)


def draw_hidden_in(key, part):
    key = jax.random.fold_in(key, 13)
    first_key, second_key, third_key = jax.random.split(key, 3)
    row_scale = jnp.exp(jax.random.uniform(first_key, (ROWS, 1), jnp.float32, math.log(0.3), math.log(3.0)))
    col_scale = jnp.exp(jax.random.uniform(second_key, (1, D), jnp.float32, math.log(0.3), math.log(3.0)))
    drawn = jax.random.truncated_normal(third_key, -4.0, 4.0, (ROWS, D), jnp.float32)
    return (drawn * row_scale * col_scale).astype(jnp.bfloat16)


def steps_of(key, dims, shards, smallest, top_value):
    gain, own = 1.0, jax.random.fold_in(key, 6)
    for axis_at, shards_of in shards:
        heights = jnp.exp(jax.random.uniform(jax.random.fold_in(own, axis_at), (shards_of,), jnp.float32, smallest / len(shards), top_value / len(shards)))
        gain = gain * jnp.repeat(heights, dims[axis_at] // shards_of).reshape([-1 if axis == axis_at else 1 for axis in range(len(dims))])
    return gain


def normal_values(rng, extent, width, reach, cuts=(), held_as=jnp.bfloat16):
    result = jax.random.normal(rng, extent, jnp.float32) * width
    if len(cuts) > 0:
        result = steps_of(rng, extent, cuts, -0.22, 0.18) * result
    return jnp.clip(result, min=-reach, max=reach).astype(held_as)


def setup_inputs(seed: int = 0) -> dict:
    keys = jax.random.split(jax.random.key(seed), 11)
    return {
        "hidden_in": draw_hidden_in(jax.random.fold_in(keys[10], 71), 0),
        "queries": draw_queries(jax.random.fold_in(keys[10], 71), 0),
        "key_cache": draw_key_cache(jax.random.fold_in(keys[10], 71), 0),
        "value_cache": normal_values(keys[3], (ROWS, KV_WIDTH), 1.0, 4.0, ((0, 4),)),
        "question": draw_question(jax.random.fold_in(keys[10], 71), 0),
        "prefix_len": draw_prefix_len(jax.random.fold_in(keys[10], 71), 0),
        "norm_gain": jnp.clip(1.0 + 0.18 * jax.random.normal(keys[6], (D,), jnp.float32), 0.1, 1.9),
        "gate_weight": normal_values(keys[7], (D, FF), D ** -0.5, 0.046875, ((0, 4), (1, 8))),
        "up_weight": normal_values(keys[8], (D, FF), D ** -0.5, 0.046875, ((0, 4), (1, 8))),
        "down_weight": normal_values(keys[9], (FF, D), FF ** -0.5, 0.0390625, ((0, 8), (1, 4))),
    }


def attend(batch_index, query_block, key_cache, value_cache, question, prefix_len):
    group_size = HEADS // KV_HEADS
    total_rows = key_cache.shape[0]
    local_rows = jnp.arange(ROWS_DEV, dtype=jnp.int32)
    option_owner = lax.dynamic_slice_in_dim(question, (batch_index * OPT_DEV).astype(jnp.int32), OPT_DEV)
    owner_rows = jnp.concatenate([jnp.zeros((PREFIX,), jnp.int32) + batch_index, option_owner.astype(jnp.int32)])
    owner_length = prefix_len[owner_rows]
    key_limit = jnp.where(local_rows < PREFIX, jnp.minimum(local_rows + 1, owner_length), owner_length)
    key_index = jnp.arange(total_rows, dtype=jnp.int32)
    key_batch = key_index // ROWS_DEV
    key_local = key_index % ROWS_DEV
    own_index = batch_index * ROWS_DEV + local_rows
    allowed = (key_batch[None, :] == owner_rows[:, None]) & (key_local[None, :] < key_limit[:, None]) | (key_index[None, :] == own_index[:, None]) & (local_rows[:, None] >= PREFIX)
    query_heads = query_block.astype(jnp.float32).reshape(ROWS_DEV, KV_HEADS, group_size, HEAD_DIM)
    key_heads = key_cache.astype(jnp.float32).reshape(total_rows, KV_HEADS, HEAD_DIM)
    value_heads = value_cache.astype(jnp.float32).reshape(total_rows, KV_HEADS, HEAD_DIM)
    scores = jnp.einsum('rgpd,kgd->gprk', query_heads, key_heads) / jnp.sqrt(jnp.float32(HEAD_DIM))
    scores = jnp.where(allowed[None, None], scores, jnp.float32(-1e+30))
    row_peak = lax.optimization_barrier(jnp.max(scores, axis=-1, keepdims=True))
    exponent = jnp.exp(scores - row_peak)
    attention = (exponent / lax.optimization_barrier(jnp.sum(exponent, axis=-1, keepdims=True))).astype(jnp.bfloat16)
    context = jnp.einsum('gprk,kgd->rgpd', attention.astype(jnp.float32), value_heads)
    return context.reshape(ROWS_DEV, D).astype(jnp.bfloat16)

def reference(hidden_in, queries, key_cache, value_cache, question, prefix_len, norm_gain, gate_weight, up_weight, down_weight):
    query_blocks = queries.reshape(QUESTIONS, ROWS_DEV, D)

    def one_block(pair):
        return attend(pair[0], pair[1], key_cache, value_cache, question, prefix_len)
    context = lax.map(one_block, (jnp.arange(QUESTIONS, dtype=jnp.int32), query_blocks)).reshape(ROWS, D)
    residual = (hidden_in.astype(jnp.float32) + context.astype(jnp.float32)).astype(jnp.bfloat16)
    widened = residual.astype(jnp.float32)
    mean_square = lax.optimization_barrier(jnp.mean(widened * widened, axis=-1, keepdims=True))
    normed = (widened * lax.rsqrt(mean_square + 1e-05) * norm_gain).astype(jnp.bfloat16)
    gate = jnp.dot(normed, gate_weight, preferred_element_type=jnp.float32)
    up_part = jnp.dot(normed, up_weight, preferred_element_type=jnp.float32)
    hidden = (jax.nn.silu(gate) * up_part).astype(jnp.bfloat16)
    branch_out = jnp.dot(hidden, down_weight, preferred_element_type=jnp.float32)
    return (residual.astype(jnp.float32) + branch_out).astype(jnp.bfloat16)
```

```python
import functools

import jax
import jax.numpy as jnp
from jax import lax
from jax.experimental import pallas as pl
from jax.experimental.pallas import tpu as pltpu
from jax.sharding import PartitionSpec as P

HEADS = 128
KV_HEADS = 8
HEAD_DIM = 128
PREFIX = 24
ROWS_DEV = 32
CHUNKS = 13
LAG = 2
GATE_SLOTS = 8
DOWN_SLOTS = 4
BLOCKS = 4
MESH = pl.DeviceIdType.MESH
F32 = jnp.float32
BF16 = jnp.bfloat16


def aligned(start, size, step=128):
    return pl.ds(pl.multiple_of(start, step), size)


def kernel(
    nb, nm,
    hidden_hbm, query_hbm, key_hbm, value_hbm, question, prefix_len, gain_hbm,
    gate_hbm, up_hbm, down_hbm,
    out_ref,
    gate_buf, up_buf, down_buf, query, hidden, keys, values, gain, own, res, normed,
    squares, squares_in, inverse, part, rs_out, rs_in, hid, acc,
    sib_out, sib_in, chip_out, chip_in,
    gate_sem, up_sem, down_sem, local_sem, kv_send, kv_recv, a_send, a_recv,
    b_send, b_recv, s_send, s_recv, sq_send, sq_recv, rs_send, rs_recv, ag_send, ag_recv,
    sib_send, sib_recv, chip_send, chip_recv,
):
    b, m = lax.axis_index("batch"), lax.axis_index("mp")
    core, chip, chips = m % 2, m // 2, nm // 2
    rows, features = res.shape
    columns = own.shape[1]
    ratio = features // columns
    half = rows // 2
    width = hid.shape[2]
    mine = rows // nm
    sibling = chip * 2 + 1 - core
    last = nb - 1

    def remote(src, dst, send, recv, to_b, to_m):
        return pltpu.make_async_remote_copy(
            src_ref=src, dst_ref=dst, send_sem=send, recv_sem=recv,
            device_id=(to_b, to_m), device_id_type=MESH,
        )

    def gate_copy(k):
        slot = k % GATE_SLOTS
        at = aligned(k * width, width)
        return (
            pltpu.make_async_copy(gate_hbm.at[:, at], gate_buf.at[slot], gate_sem.at[slot]),
            pltpu.make_async_copy(up_hbm.at[:, at], up_buf.at[slot], up_sem.at[slot]),
        )

    def down_copy(k):
        slot = k % DOWN_SLOTS
        return pltpu.make_async_copy(
            down_hbm.at[aligned(k * width, width)], down_buf.at[slot], down_sem.at[slot]
        )

    group = m * (columns // HEAD_DIM) // (HEADS // KV_HEADS)
    head_at = aligned(group * HEAD_DIM, HEAD_DIM)
    own_rows = aligned(b * ROWS_DEV, ROWS_DEV, ROWS_DEV)
    local = [
        pltpu.make_async_copy(query_hbm, query, local_sem.at[0]),
        pltpu.make_async_copy(
            hidden_hbm.at[:, aligned(m * columns, columns)], hidden, local_sem.at[1]
        ),
        pltpu.make_async_copy(
            gain_hbm.at[:, aligned(b * features, features)], gain, local_sem.at[2]
        ),
        pltpu.make_async_copy(key_hbm.at[:, head_at], keys.at[own_rows], local_sem.at[3]),
        pltpu.make_async_copy(value_hbm.at[:, head_at], values.at[own_rows], local_sem.at[4]),
    ]
    for copy in local:
        copy.start()

    barrier = pltpu.get_barrier_semaphore()

    def greet(to_b, to_m):
        pl.semaphore_signal(barrier, inc=1, device_id=(to_b, to_m), device_id_type=MESH)

    for i in range(1, nb):
        greet((b + i) % nb, m)
    for i in range(1, chips):
        greet(b, ((chip + i) % chips) * 2 + core)
    greet(b, sibling)
    own_feature = m // ratio == b
    if ratio == 2:
        senders = [(i, b * 2 + core) for i in range(nb)]
        targets = chips
    else:
        senders = [(i, b) for i in range(nb)]
        targets = nm
    for from_b, from_m in senders:
        @pl.when(jnp.logical_not(jnp.logical_and(from_b == b, from_m == m)))
        def _(from_b=from_b, from_m=from_m):
            greet(from_b, from_m)
    pl.semaphore_wait(barrier, (nb - 1) + (chips - 1) + 1 + targets - own_feature.astype(jnp.int32))

    kv = []
    for i in range(1, nb):
        for which, (src, dst) in enumerate(((key_hbm, keys), (value_hbm, values))):
            copy = remote(
                src.at[:, head_at], dst.at[own_rows],
                kv_send.at[which, i], kv_recv.at[which, i], (b + i) % nb, m,
            )
            copy.start()
            kv.append(copy)

    def start_gate(k, carry):
        for copy in gate_copy(k):
            copy.start()
        return carry

    def start_down(k, carry):
        down_copy(k).start()
        return carry

    lax.fori_loop(0, GATE_SLOTS, start_gate, 0)
    lax.fori_loop(0, DOWN_SLOTS, start_down, 0)

    acc[...] = jnp.zeros_like(acc)

    row = lax.broadcasted_iota(jnp.int32, (ROWS_DEV, rows), 0)
    key_index = lax.broadcasted_iota(jnp.int32, (ROWS_DEV, rows), 1)
    owner = jnp.zeros((ROWS_DEV, rows), jnp.int32) + b
    for i in range(ROWS_DEV - PREFIX):
        owner = jnp.where(row == PREFIX + i, question[i], owner)
    length = jnp.zeros((ROWS_DEV, rows), jnp.int32)
    for i in range(nb):
        length = jnp.where(owner == i, prefix_len[i], length)
    limit = jnp.where(row < PREFIX, jnp.minimum(row + 1, length), length)
    key_start = owner * ROWS_DEV
    allowed = ((key_index >= key_start) & (key_index < key_start + limit)) | (
        (key_index == b * ROWS_DEV + row) & (row >= PREFIX)
    )
    for copy in local:
        copy.wait()
    for copy in kv:
        copy.wait_recv()
    heads = columns // HEAD_DIM
    stacked = jnp.concatenate(
        [query[:, h * HEAD_DIM : (h + 1) * HEAD_DIM] for h in range(heads)], axis=0
    )
    scores = lax.dot_general(
        stacked, keys[...], (((1,), (1,)), ((), ())), preferred_element_type=F32
    ) * F32(HEAD_DIM**-0.5)
    scores = jnp.where(allowed[None], scores.reshape(heads, ROWS_DEV, rows), F32(-1e30))
    exponent = jnp.exp(scores - jnp.max(scores, axis=-1, keepdims=True))
    attention = exponent / jnp.sum(exponent, axis=-1, keepdims=True)
    context = jnp.dot(
        attention.reshape(heads * ROWS_DEV, rows).astype(BF16), values[...],
        preferred_element_type=F32,
    ).astype(BF16)
    for h in range(heads):
        at = slice(h * HEAD_DIM, (h + 1) * HEAD_DIM)
        own[:, at] = (
            hidden[:, at].astype(F32)
            + context[h * ROWS_DEV : (h + 1) * ROWS_DEV].astype(F32)
        ).astype(BF16)

    squares[...] = jnp.zeros_like(squares)

    def digest(at, size):
        value = res[:, at].astype(F32)
        square = value * value
        total = squares[...]
        for i in range(size // 128):
            total = total + square[:, i * 128 : (i + 1) * 128]
        squares[...] = total
        normed[:, at] = (value * gain[:, at]).astype(BF16)

    if ratio == 2:
        piece = columns // chips
        a_copies = []
        for p in range(chips):
            at = aligned(core * columns + p * piece, piece)
            here = jnp.logical_and(own_feature, chip == p)
            copy = remote(
                own.at[:, p * piece : (p + 1) * piece], res.at[own_rows, at],
                a_send.at[p], a_recv.at[b], chip, p * 2 + core,
            )
            a_copies.append((copy, here))

            @pl.when(jnp.logical_not(here))
            def _(copy=copy):
                copy.start()

            @pl.when(here)
            def _(p=p, at=at):
                res[own_rows, at] = own[:, p * piece : (p + 1) * piece]

        def region(owner_core, owner_chip):
            return aligned(owner_core * columns + owner_chip * piece, piece)

        my_at = region(core, chip)
        for i in range(nb):
            @pl.when(jnp.logical_not(jnp.logical_and(own_feature, b == i)))
            def _(i=i):
                spot = res.at[pl.ds(i * ROWS_DEV, ROWS_DEV), my_at]
                remote(spot, spot, a_send.at[0], a_recv.at[i], b, sibling).wait_recv()

        b_copies, s_copies = [], []
        for i in range(1, chips):
            copy = remote(
                res.at[:, my_at], res.at[:, my_at], b_send.at[i], b_recv.at[i],
                b, ((chip + i) % chips) * 2 + core,
            )
            copy.start()
            b_copies.append(copy)
        copy = remote(res.at[:, my_at], res.at[:, my_at], s_send.at[0], s_recv.at[0], b, sibling)
        copy.start()
        s_copies.append(copy)
        digest(my_at, piece)
        for i in range(1, chips):
            at = region(core, (chip + chips - i) % chips)
            spot = res.at[:, at]
            remote(spot, spot, b_send.at[i], b_recv.at[i], b, sibling).wait_recv()
            copy = remote(spot, spot, s_send.at[i], s_recv.at[i], b, sibling)
            copy.start()
            s_copies.append(copy)
            digest(at, piece)
        for i in range(chips):
            at = region(1 - core, (chip + chips - i) % chips)
            spot = res.at[:, at]
            remote(spot, spot, s_send.at[i], s_recv.at[i], b, sibling).wait_recv()
            digest(at, piece)
    else:
        a_copies, b_copies, s_copies = [], [], []
        for j in range(nm):
            here = jnp.logical_and(own_feature, m == j)
            copy = remote(own, res.at[own_rows], a_send.at[j], a_recv.at[b], m, j)
            a_copies.append((copy, here))

            @pl.when(jnp.logical_not(here))
            def _(copy=copy):
                copy.start()

            @pl.when(here)
            def _():
                res[own_rows, :] = own[...]

        for i in range(nb):
            @pl.when(jnp.logical_not(jnp.logical_and(own_feature, b == i)))
            def _(i=i):
                spot = res.at[pl.ds(i * ROWS_DEV, ROWS_DEV)]
                remote(spot, spot, a_send.at[0], a_recv.at[i], b, sibling).wait_recv()

        digest(slice(0, features), features)

    ends = ((0, 0), (1, last))
    sq_copies = []
    for way, end in ends:
        copy = remote(
            squares.at[pl.ds(way * half, half)], squares_in.at[b],
            sq_send.at[way], sq_recv.at[b], end, m,
        )
        sq_copies.append((copy, end))

        @pl.when(b != end)
        def _(copy=copy):
            copy.start()

    def finish_squares(way, end):
        total = squares[way * half : (way + 1) * half]
        for i in range(nb):
            if i != end:
                remote(
                    squares_in.at[i], squares_in.at[i], sq_send.at[way], sq_recv.at[i], b, sibling
                ).wait_recv()
                total = total + squares_in[i]
        mean = jnp.sum(total, axis=-1, keepdims=True) / F32(features * nb)
        inverse[...] = jnp.broadcast_to(lax.rsqrt(mean + F32(1e-05)), inverse.shape)

    def rs_copy(way, k):
        to_b = jnp.maximum(b - 1, 0) if way == 0 else jnp.minimum(b + 1, last)
        return remote(
            rs_out.at[way, k], rs_in.at[way, k], rs_send.at[way, k], rs_recv.at[way, k], to_b, m
        )

    def ag_copy(way, k):
        to_b = jnp.minimum(b + 1, last) if way == 0 else jnp.maximum(b - 1, 0)
        spot = hid.at[k, pl.ds(way * half, half)]
        return remote(spot, spot, ag_send.at[way, k], ag_recv.at[way, k], to_b, m)

    def reduce_step(way, k):
        at = slice(way * half, (way + 1) * half)
        start, end = (last, 0) if way == 0 else (0, last)

        @pl.when(b == start)
        def _():
            rs_out[way, k] = part[k, at].astype(BF16)
            rs_copy(way, k).start()

        @pl.when(jnp.logical_and(b != start, b != end))
        def _():
            rs_copy(way, k).wait_recv()
            rs_out[way, k] = (part[k, at] + rs_in[way, k].astype(F32)).astype(BF16)
            rs_copy(way, k).start()

        @pl.when(b == end)
        def _():
            @pl.when(k == 0)
            def _():
                finish_squares(way, end)

            rs_copy(way, k).wait_recv()
            scale = inverse[:, :1]
            gate = (part[k, at, :width] + rs_in[way, k, :, :width].astype(F32)) * scale
            up = (part[k, at, width:] + rs_in[way, k, :, width:].astype(F32)) * scale
            hid[k, at] = (gate / (F32(1) + jnp.exp(-gate)) * up).astype(BF16)
            ag_copy(way, k).start()

    def gather_step(way, k):
        ag_copy(way, k).wait_recv()

        @pl.when(b != (last if way == 0 else 0))
        def _():
            ag_copy(way, k).start()

    def inside(k):
        return jnp.logical_and(k >= 0, k < CHUNKS)

    def step(t, carry):
        @pl.when(t < CHUNKS)
        def _():
            slot = t % GATE_SLOTS
            gate_wait, up_wait = gate_copy(t)
            gate_wait.wait()
            part[t, :, :width] = jnp.dot(
                normed[...], gate_buf[slot], preferred_element_type=F32
            )
            up_wait.wait()
            part[t, :, width:] = jnp.dot(
                normed[...], up_buf[slot], preferred_element_type=F32
            )

            @pl.when(t + GATE_SLOTS < CHUNKS)
            def _():
                start_gate(t + GATE_SLOTS, 0)

        for way in range(2):
            hops = last - b if way == 0 else b
            k = t - hops * LAG

            @pl.when(inside(k))
            def _(way=way, k=k):
                reduce_step(way, k)

        for way in range(2):
            hops = b if way == 0 else last - b
            k = t - (last + hops) * LAG

            @pl.when(jnp.logical_and(inside(k), hops > 0))
            def _(way=way, k=k):
                gather_step(way, k)

        k = t - (last + jnp.maximum(b, last - b)) * LAG

        @pl.when(inside(k))
        def _():
            down_copy(k).wait()
            tile = min(512, features)
            for j in range(features // tile):
                at = slice(j * tile, (j + 1) * tile)
                acc[:, at] += jnp.dot(
                    hid[k], down_buf[k % DOWN_SLOTS, :, at], preferred_element_type=F32
                )

            @pl.when(k + DOWN_SLOTS < CHUNKS)
            def _():
                start_down(k + DOWN_SLOTS, 0)

        return carry

    lax.fori_loop(0, CHUNKS + 2 * last * LAG, step, 0)

    block = features // BLOCKS
    sib_copies, chip_copies = [], []

    def rows_of(p, c):
        return pl.ds(pl.multiple_of((p * 2 + c) * mine, mine), mine)

    for j in range(BLOCKS):
        at = slice(j * block, (j + 1) * block)
        for p in range(chips):
            sib_out[j, p] = acc[rows_of(p, 1 - core), at].astype(BF16)
        copy = remote(sib_out.at[j], sib_in.at[j], sib_send.at[j], sib_recv.at[j], b, sibling)
        copy.start()
        sib_copies.append(copy)
    for j in range(BLOCKS):
        at = slice(j * block, (j + 1) * block)
        sib_copies[j].wait_recv()
        for i in range(1, chips):
            to = (chip + i) % chips
            chip_out[j, i] = (
                acc[rows_of(to, core), at] + sib_in[j, to].astype(F32)
            ).astype(BF16)
            copy = remote(
                chip_out.at[j, i], chip_in.at[j, i], chip_send.at[j, i], chip_recv.at[j, i],
                b, to * 2 + core,
            )
            copy.start()
            chip_copies.append(copy)
    for j in range(BLOCKS):
        at = slice(j * block, (j + 1) * block)
        total = acc[rows_of(chip, core), at] + sib_in[j, chip].astype(F32)
        for i in range(1, chips):
            chip_copies[j * (chips - 1) + i - 1].wait_recv()
            total = total + chip_in[j, i].astype(F32)
        out_ref[:, at] = (res[rows_of(chip, core), at].astype(F32) + total).astype(BF16)

    for copy in kv + b_copies + s_copies + sib_copies + chip_copies:
        copy.wait_send()
    for copy, here in a_copies:
        @pl.when(jnp.logical_not(here))
        def _(copy=copy):
            copy.wait_send()
    for copy, end in sq_copies:
        @pl.when(b != end)
        def _(copy=copy):
            copy.wait_send()

    def drain(k, carry):
        for way in range(2):
            stop = 0 if way == 0 else last

            @pl.when(b != stop)
            def _(way=way):
                rs_copy(way, k).wait_send()

            @pl.when(b != last - stop)
            def _(way=way):
                ag_copy(way, k).wait_send()
        return carry

    lax.fori_loop(0, CHUNKS, drain, 0)


def body(
    nb, nm, hidden_in, queries, key_cache, value_cache, question, prefix_len, norm_gain,
    gate_weight, up_weight, down_weight,
):
    features, units = gate_weight.shape
    columns = queries.shape[1]
    rows = nb * ROWS_DEV
    width, half, chips, mine = units // CHUNKS, rows // 2, nm // 2, rows // nm
    block = features // BLOCKS
    dma = pltpu.SemaphoreType.DMA
    scratch = [
        pltpu.VMEM((GATE_SLOTS, features, width), BF16),
        pltpu.VMEM((GATE_SLOTS, features, width), BF16),
        pltpu.VMEM((DOWN_SLOTS, width, features), BF16),
        pltpu.VMEM((ROWS_DEV, columns), BF16),
        pltpu.VMEM((ROWS_DEV, columns), BF16),
        pltpu.VMEM((rows, HEAD_DIM), BF16),
        pltpu.VMEM((rows, HEAD_DIM), BF16),
        pltpu.VMEM((1, features), F32),
        pltpu.VMEM((ROWS_DEV, columns), BF16),
        pltpu.VMEM((rows, features), BF16),
        pltpu.VMEM((rows, features), BF16),
        pltpu.VMEM((rows, 128), F32),
        pltpu.VMEM((nb, half, 128), F32),
        pltpu.VMEM((half, 128), F32),
        pltpu.VMEM((CHUNKS, rows, 2 * width), F32),
        pltpu.VMEM((2, CHUNKS, half, 2 * width), BF16),
        pltpu.VMEM((2, CHUNKS, half, 2 * width), BF16),
        pltpu.VMEM((CHUNKS, rows, width), BF16),
        pltpu.VMEM((rows, features), F32),
        pltpu.VMEM((BLOCKS, chips, mine, block), BF16),
        pltpu.VMEM((BLOCKS, chips, mine, block), BF16),
        pltpu.VMEM((BLOCKS, chips, mine, block), BF16),
        pltpu.VMEM((BLOCKS, chips, mine, block), BF16),
        dma((GATE_SLOTS,)), dma((GATE_SLOTS,)), dma((DOWN_SLOTS,)), dma((5,)),
        dma((2, nb)), dma((2, nb)), dma((nm,)), dma((nb,)),
        dma((chips,)), dma((chips,)), dma((chips,)), dma((chips,)),
        dma((2,)), dma((nb,)),
        dma((2, CHUNKS)), dma((2, CHUNKS)), dma((2, CHUNKS)), dma((2, CHUNKS)),
        dma((BLOCKS,)), dma((BLOCKS,)), dma((BLOCKS, chips)), dma((BLOCKS, chips)),
    ]
    anywhere = pl.BlockSpec(memory_space=pl.ANY)
    scalars = pl.BlockSpec(memory_space=pltpu.SMEM)
    return pl.pallas_call(
        functools.partial(kernel, nb, nm),
        out_shape=jax.ShapeDtypeStruct((mine, features), BF16),
        in_specs=[anywhere] * 4 + [scalars] * 2 + [anywhere] * 4,
        out_specs=pl.BlockSpec(memory_space=pltpu.VMEM),
        scratch_shapes=scratch,
        compiler_params=pltpu.CompilerParams(
            collective_id=0, has_side_effects=True, vmem_limit_bytes=60 * 2**20
        ),
        cost_estimate=pl.CostEstimate(
            flops=6 * rows * features * units, bytes_accessed=6 * features * units,
            transcendentals=0,
        ),
    )(
        hidden_in, queries, key_cache, value_cache, question, prefix_len,
        norm_gain.reshape(1, -1), gate_weight, up_weight, down_weight,
    )


def solution(mesh):
    return jax.shard_map(
        functools.partial(body, mesh.shape["batch"], mesh.shape["mp"]),
        mesh=mesh,
        in_specs=(
            P("batch", None),
            P("batch", "mp"),
            P("batch", None),
            P("batch", None),
            P("batch"),
            P(),
            P(),
            P("batch", "mp"),
            P("batch", "mp"),
            P("mp", "batch"),
        ),
        out_specs=P("mp", "batch"),
        check_vma=False,
    )
```

```python
import functools

import jax
import jax.numpy as jnp
from jax import lax
from jax.experimental import pallas as pl
from jax.experimental.pallas import tpu as pltpu
from jax.sharding import PartitionSpec as P

HEADS = 128
KV_HEADS = 8
HEAD_DIM = 128
PREFIX = 24
ROWS_DEV = 32
CHUNKS = 13
LAG = 2
GATE_SLOTS = 8
DOWN_SLOTS = 4
BLOCKS = 4
MESH = pl.DeviceIdType.MESH
F32 = jnp.float32
BF16 = jnp.bfloat16


def aligned(start, size, step=128):
    return pl.ds(pl.multiple_of(start, step), size)


def kernel(
    nb, nm,
    hidden_hbm, query_hbm, key_hbm, value_hbm, question, prefix_len, gain_hbm,
    gate_hbm, up_hbm, down_hbm,
    out_ref,
    gate_buf, up_buf, down_buf, query, hidden, keys, values, gain, own, res, normed,
    squares, squares_in, inverse, part, rs_out, rs_in, hid, acc,
    sib_out, sib_in, chip_out, chip_in,
    gate_sem, up_sem, down_sem, local_sem, kv_send, kv_recv, a_send, a_recv,
    b_send, b_recv, s_send, s_recv, sq_send, sq_recv, rs_send, rs_recv, ag_send, ag_recv,
    sib_send, sib_recv, chip_send, chip_recv,
):
    b, m = lax.axis_index("batch"), lax.axis_index("mp")
    core, chip, chips = m % 2, m // 2, nm // 2
    rows, features = res.shape
    columns = own.shape[1]
    ratio = features // columns
    half = rows // 2
    width = hid.shape[2]
    mine = rows // nm
    sibling = chip * 2 + 1 - core
    last = nb - 1

    def remote(src, dst, send, recv, to_b, to_m):
        return pltpu.make_async_remote_copy(
            src_ref=src, dst_ref=dst, send_sem=send, recv_sem=recv,
            device_id=(to_b, to_m), device_id_type=MESH,
        )

    def gate_copy(k):
        slot = k % GATE_SLOTS
        at = aligned(k * width, width)
        return (
            pltpu.make_async_copy(gate_hbm.at[:, at], gate_buf.at[slot], gate_sem.at[slot]),
            pltpu.make_async_copy(up_hbm.at[:, at], up_buf.at[slot], up_sem.at[slot]),
        )

    def down_copy(k):
        slot = k % DOWN_SLOTS
        return pltpu.make_async_copy(
            down_hbm.at[aligned(k * width, width)], down_buf.at[slot], down_sem.at[slot]
        )

    group = m * (columns // HEAD_DIM) // (HEADS // KV_HEADS)
    head_at = aligned(group * HEAD_DIM, HEAD_DIM)
    own_rows = aligned(b * ROWS_DEV, ROWS_DEV, ROWS_DEV)
    local = [
        pltpu.make_async_copy(query_hbm, query, local_sem.at[0]),
        pltpu.make_async_copy(
            hidden_hbm.at[:, aligned(m * columns, columns)], hidden, local_sem.at[1]
        ),
        pltpu.make_async_copy(
            gain_hbm.at[:, aligned(b * features, features)], gain, local_sem.at[2]
        ),
        pltpu.make_async_copy(key_hbm.at[:, head_at], keys.at[own_rows], local_sem.at[3]),
        pltpu.make_async_copy(value_hbm.at[:, head_at], values.at[own_rows], local_sem.at[4]),
    ]
    for copy in local:
        copy.start()

    barrier = pltpu.get_barrier_semaphore()

    def greet(to_b, to_m):
        pl.semaphore_signal(barrier, inc=1, device_id=(to_b, to_m), device_id_type=MESH)

    for i in range(1, nb):
        greet((b + i) % nb, m)
    for i in range(1, chips):
        greet(b, ((chip + i) % chips) * 2 + core)
    greet(b, sibling)
    own_feature = m // ratio == b
    if ratio == 2:
        senders = [(i, b * 2 + core) for i in range(nb)]
        targets = chips
    else:
        senders = [(i, b) for i in range(nb)]
        targets = nm
    for from_b, from_m in senders:
        @pl.when(jnp.logical_not(jnp.logical_and(from_b == b, from_m == m)))
        def _(from_b=from_b, from_m=from_m):
            greet(from_b, from_m)
    pl.semaphore_wait(barrier, (nb - 1) + (chips - 1) + 1 + targets - own_feature.astype(jnp.int32))

    kv = []
    for i in range(1, nb):
        for which, (src, dst) in enumerate(((key_hbm, keys), (value_hbm, values))):
            copy = remote(
                src.at[:, head_at], dst.at[own_rows],
                kv_send.at[which, i], kv_recv.at[which, i], (b + i) % nb, m,
            )
            copy.start()
            kv.append(copy)

    def start_gate(k, carry):
        for copy in gate_copy(k):
            copy.start()
        return carry

    def start_down(k, carry):
        down_copy(k).start()
        return carry

    lax.fori_loop(0, GATE_SLOTS, start_gate, 0)
    lax.fori_loop(0, DOWN_SLOTS, start_down, 0)

    acc[...] = jnp.zeros_like(acc)

    row = lax.broadcasted_iota(jnp.int32, (ROWS_DEV, rows), 0)
    key_index = lax.broadcasted_iota(jnp.int32, (ROWS_DEV, rows), 1)
    owner = jnp.zeros((ROWS_DEV, rows), jnp.int32) + b
    for i in range(ROWS_DEV - PREFIX):
        owner = jnp.where(row == PREFIX + i, question[i], owner)
    length = jnp.zeros((ROWS_DEV, rows), jnp.int32)
    for i in range(nb):
        length = jnp.where(owner == i, prefix_len[i], length)
    limit = jnp.where(row < PREFIX, jnp.minimum(row + 1, length), length)
    key_start = owner * ROWS_DEV
    allowed = ((key_index >= key_start) & (key_index < key_start + limit)) | (
        (key_index == b * ROWS_DEV + row) & (row >= PREFIX)
    )
    for copy in local:
        copy.wait()
    for copy in kv:
        copy.wait_recv()
    heads = columns // HEAD_DIM
    stacked = jnp.concatenate(
        [query[:, h * HEAD_DIM : (h + 1) * HEAD_DIM] for h in range(heads)], axis=0
    )
    scores = lax.dot_general(
        stacked, keys[...], (((1,), (1,)), ((), ())), preferred_element_type=F32
    ) * F32(HEAD_DIM**-0.5)
    scores = jnp.where(allowed[None], scores.reshape(heads, ROWS_DEV, rows), F32(-1e30))
    exponent = jnp.exp(scores - jnp.max(scores, axis=-1, keepdims=True))
    attention = exponent / jnp.sum(exponent, axis=-1, keepdims=True)
    context = jnp.dot(
        attention.reshape(heads * ROWS_DEV, rows).astype(BF16), values[...],
        preferred_element_type=F32,
    ).astype(BF16)
    for h in range(heads):
        at = slice(h * HEAD_DIM, (h + 1) * HEAD_DIM)
        own[:, at] = (
            hidden[:, at].astype(F32)
            + context[h * ROWS_DEV : (h + 1) * ROWS_DEV].astype(F32)
        ).astype(BF16)

    squares[...] = jnp.zeros_like(squares)

    def digest(at, size):
        value = res[:, at].astype(F32)
        square = value * value
        total = squares[...]
        for i in range(size // 128):
            total = total + square[:, i * 128 : (i + 1) * 128]
        squares[...] = total
        normed[:, at] = (value * gain[:, at]).astype(BF16)

    if ratio == 2:
        piece = columns // chips
        a_copies = []
        for p in range(chips):
            at = aligned(core * columns + p * piece, piece)
            here = jnp.logical_and(own_feature, chip == p)
            copy = remote(
                own.at[:, p * piece : (p + 1) * piece], res.at[own_rows, at],
                a_send.at[p], a_recv.at[b], chip, p * 2 + core,
            )
            a_copies.append((copy, here))

            @pl.when(jnp.logical_not(here))
            def _(copy=copy):
                copy.start()

            @pl.when(here)
            def _(p=p, at=at):
                res[own_rows, at] = own[:, p * piece : (p + 1) * piece]

        def region(owner_core, owner_chip):
            return aligned(owner_core * columns + owner_chip * piece, piece)

        my_at = region(core, chip)
        b_copies, s_copies = [], []
        for ahead in range(nb):
            source = (b + ahead) % nb
            spot = res.at[aligned(source * ROWS_DEV, ROWS_DEV, ROWS_DEV), my_at]
            arrival = remote(spot, spot, a_send.at[0], a_recv.at[source], b, sibling)
            if ahead == 0:
                pl.when(jnp.logical_not(own_feature))(arrival.wait_recv)
            else:
                arrival.wait_recv()
            for i in range(1, chips):
                copy = remote(
                    spot, spot, b_send.at[ahead, i], b_recv.at[ahead, i],
                    b, ((chip + i) % chips) * 2 + core,
                )
                copy.start()
                b_copies.append(copy)
        copy = remote(res.at[:, my_at], res.at[:, my_at], s_send.at[0], s_recv.at[0], b, sibling)
        copy.start()
        s_copies.append(copy)
        digest(my_at, piece)
        for i in range(1, chips):
            at = region(core, (chip + chips - i) % chips)
            spot = res.at[:, at]
            for ahead in range(nb):
                source = (b + ahead) % nb
                part_spot = res.at[aligned(source * ROWS_DEV, ROWS_DEV, ROWS_DEV), at]
                remote(
                    part_spot, part_spot, b_send.at[ahead, i], b_recv.at[ahead, i], b, sibling
                ).wait_recv()
            copy = remote(spot, spot, s_send.at[i], s_recv.at[i], b, sibling)
            copy.start()
            s_copies.append(copy)
            digest(at, piece)
        for i in range(chips):
            at = region(1 - core, (chip + chips - i) % chips)
            spot = res.at[:, at]
            remote(spot, spot, s_send.at[i], s_recv.at[i], b, sibling).wait_recv()
            digest(at, piece)
    else:
        a_copies, b_copies, s_copies = [], [], []
        for j in range(nm):
            here = jnp.logical_and(own_feature, m == j)
            copy = remote(own, res.at[own_rows], a_send.at[j], a_recv.at[b], m, j)
            a_copies.append((copy, here))

            @pl.when(jnp.logical_not(here))
            def _(copy=copy):
                copy.start()

            @pl.when(here)
            def _():
                res[own_rows, :] = own[...]

        for i in range(nb):
            @pl.when(jnp.logical_not(jnp.logical_and(own_feature, b == i)))
            def _(i=i):
                spot = res.at[pl.ds(i * ROWS_DEV, ROWS_DEV)]
                remote(spot, spot, a_send.at[0], a_recv.at[i], b, sibling).wait_recv()

        digest(slice(0, features), features)

    ends = ((0, 0), (1, last))
    sq_copies = []
    for way, end in ends:
        copy = remote(
            squares.at[pl.ds(way * half, half)], squares_in.at[b],
            sq_send.at[way], sq_recv.at[b], end, m,
        )
        sq_copies.append((copy, end))

        @pl.when(b != end)
        def _(copy=copy):
            copy.start()

    def finish_squares(way, end):
        total = squares[way * half : (way + 1) * half]
        for i in range(nb):
            if i != end:
                remote(
                    squares_in.at[i], squares_in.at[i], sq_send.at[way], sq_recv.at[i], b, sibling
                ).wait_recv()
                total = total + squares_in[i]
        mean = jnp.sum(total, axis=-1, keepdims=True) / F32(features * nb)
        inverse[...] = jnp.broadcast_to(lax.rsqrt(mean + F32(1e-05)), inverse.shape)

    def rs_copy(way, k):
        to_b = jnp.maximum(b - 1, 0) if way == 0 else jnp.minimum(b + 1, last)
        return remote(
            rs_out.at[way, k], rs_in.at[way, k], rs_send.at[way, k], rs_recv.at[way, k], to_b, m
        )

    def ag_copy(way, k):
        to_b = jnp.minimum(b + 1, last) if way == 0 else jnp.maximum(b - 1, 0)
        spot = hid.at[k, pl.ds(way * half, half)]
        return remote(spot, spot, ag_send.at[way, k], ag_recv.at[way, k], to_b, m)

    def reduce_step(way, k):
        at = slice(way * half, (way + 1) * half)
        start, end = (last, 0) if way == 0 else (0, last)

        @pl.when(b == start)
        def _():
            rs_out[way, k] = part[k, at].astype(BF16)
            rs_copy(way, k).start()

        @pl.when(jnp.logical_and(b != start, b != end))
        def _():
            rs_copy(way, k).wait_recv()
            rs_out[way, k] = (part[k, at] + rs_in[way, k].astype(F32)).astype(BF16)
            rs_copy(way, k).start()

        @pl.when(b == end)
        def _():
            @pl.when(k == 0)
            def _():
                finish_squares(way, end)

            rs_copy(way, k).wait_recv()
            scale = inverse[:, :1]
            gate = (part[k, at, :width] + rs_in[way, k, :, :width].astype(F32)) * scale
            up = (part[k, at, width:] + rs_in[way, k, :, width:].astype(F32)) * scale
            hid[k, at] = (gate / (F32(1) + jnp.exp(-gate)) * up).astype(BF16)
            ag_copy(way, k).start()

    def gather_step(way, k):
        ag_copy(way, k).wait_recv()

        @pl.when(b != (last if way == 0 else 0))
        def _():
            ag_copy(way, k).start()

    block = features // BLOCKS

    def rows_of(p, c):
        return pl.ds(pl.multiple_of((p * 2 + c) * mine, mine), mine)

    def sib_copy(j):
        return remote(sib_out.at[j], sib_in.at[j], sib_send.at[j], sib_recv.at[j], b, sibling)

    def send_sibling(j):
        at = slice(j * block, (j + 1) * block)
        for p in range(chips):
            sib_out[j, p] = acc[rows_of(p, 1 - core), at].astype(BF16)
        sib_copy(j).start()

    def inside(k):
        return jnp.logical_and(k >= 0, k < CHUNKS)

    def step(t, carry):
        @pl.when(t < CHUNKS)
        def _():
            slot = t % GATE_SLOTS
            gate_wait, up_wait = gate_copy(t)
            gate_wait.wait()
            part[t, :, :width] = jnp.dot(
                normed[...], gate_buf[slot], preferred_element_type=F32
            )
            up_wait.wait()
            part[t, :, width:] = jnp.dot(
                normed[...], up_buf[slot], preferred_element_type=F32
            )

            @pl.when(t + GATE_SLOTS < CHUNKS)
            def _():
                start_gate(t + GATE_SLOTS, 0)

        for way in range(2):
            hops = last - b if way == 0 else b
            k = t - hops * LAG

            @pl.when(inside(k))
            def _(way=way, k=k):
                reduce_step(way, k)

        for way in range(2):
            hops = b if way == 0 else last - b
            k = t - (last + hops) * LAG

            @pl.when(jnp.logical_and(inside(k), hops > 0))
            def _(way=way, k=k):
                gather_step(way, k)

        k = t - (last + jnp.maximum(b, last - b)) * LAG

        @pl.when(inside(k))
        def _():
            down_copy(k).wait()
            tile = min(512, features)
            for j in range(features // tile):
                at = slice(j * tile, (j + 1) * tile)
                acc[:, at] += jnp.dot(
                    hid[k], down_buf[k % DOWN_SLOTS, :, at], preferred_element_type=F32
                )
                ready = [
                    i for i in range(BLOCKS) if j * tile < (i + 1) * block <= (j + 1) * tile
                ]
                if ready:
                    @pl.when(k == CHUNKS - 1)
                    def _(ready=ready):
                        for i in ready:
                            send_sibling(i)

            @pl.when(k + DOWN_SLOTS < CHUNKS)
            def _():
                start_down(k + DOWN_SLOTS, 0)

        return carry

    lax.fori_loop(0, CHUNKS + 2 * last * LAG, step, 0)

    sib_copies, chip_copies = [sib_copy(j) for j in range(BLOCKS)], []

    for j in range(BLOCKS):
        at = slice(j * block, (j + 1) * block)
        sib_copies[j].wait_recv()
        for i in range(1, chips):
            to = (chip + i) % chips
            chip_out[j, i] = (
                acc[rows_of(to, core), at] + sib_in[j, to].astype(F32)
            ).astype(BF16)
            copy = remote(
                chip_out.at[j, i], chip_in.at[j, i], chip_send.at[j, i], chip_recv.at[j, i],
                b, to * 2 + core,
            )
            copy.start()
            chip_copies.append(copy)
    for j in range(BLOCKS):
        at = slice(j * block, (j + 1) * block)
        total = acc[rows_of(chip, core), at] + sib_in[j, chip].astype(F32)
        for i in range(1, chips):
            chip_copies[j * (chips - 1) + i - 1].wait_recv()
            total = total + chip_in[j, i].astype(F32)
        out_ref[:, at] = (res[rows_of(chip, core), at].astype(F32) + total).astype(BF16)

    for copy in kv + b_copies + s_copies + sib_copies + chip_copies:
        copy.wait_send()
    for copy, here in a_copies:
        @pl.when(jnp.logical_not(here))
        def _(copy=copy):
            copy.wait_send()
    for copy, end in sq_copies:
        @pl.when(b != end)
        def _(copy=copy):
            copy.wait_send()

    def drain(k, carry):
        for way in range(2):
            stop = 0 if way == 0 else last

            @pl.when(b != stop)
            def _(way=way):
                rs_copy(way, k).wait_send()

            @pl.when(b != last - stop)
            def _(way=way):
                ag_copy(way, k).wait_send()
        return carry

    lax.fori_loop(0, CHUNKS, drain, 0)


def body(
    nb, nm, hidden_in, queries, key_cache, value_cache, question, prefix_len, norm_gain,
    gate_weight, up_weight, down_weight,
):
    features, units = gate_weight.shape
    columns = queries.shape[1]
    rows = nb * ROWS_DEV
    width, half, chips, mine = units // CHUNKS, rows // 2, nm // 2, rows // nm
    block = features // BLOCKS
    dma = pltpu.SemaphoreType.DMA
    scratch = [
        pltpu.VMEM((GATE_SLOTS, features, width), BF16),
        pltpu.VMEM((GATE_SLOTS, features, width), BF16),
        pltpu.VMEM((DOWN_SLOTS, width, features), BF16),
        pltpu.VMEM((ROWS_DEV, columns), BF16),
        pltpu.VMEM((ROWS_DEV, columns), BF16),
        pltpu.VMEM((rows, HEAD_DIM), BF16),
        pltpu.VMEM((rows, HEAD_DIM), BF16),
        pltpu.VMEM((1, features), F32),
        pltpu.VMEM((ROWS_DEV, columns), BF16),
        pltpu.VMEM((rows, features), BF16),
        pltpu.VMEM((rows, features), BF16),
        pltpu.VMEM((rows, 128), F32),
        pltpu.VMEM((nb, half, 128), F32),
        pltpu.VMEM((half, 128), F32),
        pltpu.VMEM((CHUNKS, rows, 2 * width), F32),
        pltpu.VMEM((2, CHUNKS, half, 2 * width), BF16),
        pltpu.VMEM((2, CHUNKS, half, 2 * width), BF16),
        pltpu.VMEM((CHUNKS, rows, width), BF16),
        pltpu.VMEM((rows, features), F32),
        pltpu.VMEM((BLOCKS, chips, mine, block), BF16),
        pltpu.VMEM((BLOCKS, chips, mine, block), BF16),
        pltpu.VMEM((BLOCKS, chips, mine, block), BF16),
        pltpu.VMEM((BLOCKS, chips, mine, block), BF16),
        dma((GATE_SLOTS,)), dma((GATE_SLOTS,)), dma((DOWN_SLOTS,)), dma((5,)),
        dma((2, nb)), dma((2, nb)), dma((nm,)), dma((nb,)),
        dma((nb, chips)), dma((nb, chips)), dma((chips,)), dma((chips,)),
        dma((2,)), dma((nb,)),
        dma((2, CHUNKS)), dma((2, CHUNKS)), dma((2, CHUNKS)), dma((2, CHUNKS)),
        dma((BLOCKS,)), dma((BLOCKS,)), dma((BLOCKS, chips)), dma((BLOCKS, chips)),
    ]
    anywhere = pl.BlockSpec(memory_space=pl.ANY)
    scalars = pl.BlockSpec(memory_space=pltpu.SMEM)
    return pl.pallas_call(
        functools.partial(kernel, nb, nm),
        out_shape=jax.ShapeDtypeStruct((mine, features), BF16),
        in_specs=[anywhere] * 4 + [scalars] * 2 + [anywhere] * 4,
        out_specs=pl.BlockSpec(memory_space=pltpu.VMEM),
        scratch_shapes=scratch,
        compiler_params=pltpu.CompilerParams(
            collective_id=0, has_side_effects=True, vmem_limit_bytes=60 * 2**20
        ),
        cost_estimate=pl.CostEstimate(
            flops=6 * rows * features * units, bytes_accessed=6 * features * units,
            transcendentals=0,
        ),
    )(
        hidden_in, queries, key_cache, value_cache, question, prefix_len,
        norm_gain.reshape(1, -1), gate_weight, up_weight, down_weight,
    )


def solution(mesh):
    return jax.shard_map(
        functools.partial(body, mesh.shape["batch"], mesh.shape["mp"]),
        mesh=mesh,
        in_specs=(
            P("batch", None),
            P("batch", "mp"),
            P("batch", None),
            P("batch", None),
            P("batch"),
            P(),
            P(),
            P("batch", "mp"),
            P("batch", "mp"),
            P("mp", "batch"),
        ),
        out_specs=P("mp", "batch"),
        check_vma=False,
    )
```
